32 devices in a mesh: adapter: 8 (over z, y), tensor: 4 (over x, core).
Axes of the slice: x: 2, y: 2, z: 4, core: 2. Of those that a mesh axis runs over, the one named last changes fastest.
Arguments:
- hidden: bfloat16 [768, 2, 8192], P('adapter'), may hold values from -6 to 6
- input_norm_gain: bfloat16 [8192], replicated, may hold values from 0.25 to 1.75
- key_value_weight: bfloat16 [8192, 2, 1024], P(None, None, 'tensor'), may hold values from -0.0625 to 0.0625
- adapter_down_weight: bfloat16 [32, 8192, 128], P('adapter', 'tensor'), may hold values from -0.0625 to 0.0625
- adapter_up_weight: bfloat16 [32, 2, 64, 1024], P('adapter', None, None, 'tensor'), may hold values from -0.375 to 0.375
- request_adapter: int32 [768], P('adapter'), may hold values from 0 to 31, as said below
- queries: bfloat16 [768, 2, 8192], P('adapter', None, 'tensor'), may hold values from -100 to 100
- cached_key_rows: bfloat16 [768, 64, 1024], P('adapter', None, 'tensor'), may hold values from -5 to 5
- cached_value_rows: bfloat16 [768, 64, 1024], P('adapter', None, 'tensor'), may hold values from -6 to 6
- cached_length: int32 [768], P('adapter'), may hold values from 2 to 64, as said below
Outputs:
- new_keys: bfloat16 [768, 2, 1024], P('adapter', None, 'tensor')
- new_values: bfloat16 [768, 2, 1024], P('adapter', None, 'tensor')
- attended: bfloat16 [768, 2, 8192], P('adapter', None, 'tensor')
The draws below stay inside these ranges and needn't reach their ends.
Inputs may be any that keep to these rules, and one draw needn't show every extreme that they name: `request_adapter`: adapter a is held by adapter index a // 4. Of the requests on one adapter index at most 24 name adapters held by one adapter index, and in every draw one adapter index is named by exactly 24 requests of every adapter index. `cached_length`: some request has exactly 64 cached tokens.
All inputs are finite; a program needn't handle non-finite values.
Results may differ from the reference program's by a relative error of at most 0.0055.
Values may be sent and summed in bfloat16 or wider, within the bound.
A program may use at most 128 MiB of HBM per device.

```python
import jax
import jax.numpy as jnp
from jax import lax

MODEL_DIM = 8192
KEY_VALUE_HEADS = 8
HEAD_DIM = 128
GQ = 8
ADAPTER_RANK = 64
NEW_TOKENS = 2
REQUESTS_PER_SLOT = 96
CTX = 64
AD_DEV = 4
REQUESTS = 768
ADAPTER_TOTAL = 32


def shared_keys(key):
    base_keys = jax.random.normal(jax.random.fold_in(key, 23), (REQUESTS, CTX, KEY_VALUE_HEADS * HEAD_DIM), jnp.float32)
    base_keys = jnp.clip(base_keys, -5.0, 5.0)
    return base_keys


def draw_cached_key_rows(key, part):
    return shared_keys(key).astype(jnp.bfloat16)


def draw_queries(key, part):
    fresh_draw = jax.random.normal(jax.random.fold_in(key, 24), (REQUESTS, NEW_TOKENS, KEY_VALUE_HEADS * GQ * HEAD_DIM), jnp.float32)
    fresh_draw = jnp.clip(fresh_draw, -5.0, 5.0)
    return fresh_draw.astype(jnp.bfloat16)


def draw_cached_length(key, part):
    lengths = jax.random.randint(jax.random.fold_in(key, 31), (REQUESTS,), 2, CTX + 1)
    longest = jax.random.randint(jax.random.fold_in(key, 32), (), 0, REQUESTS)
    return jnp.where(jnp.arange(REQUESTS, dtype=jnp.int32) == longest, CTX, lengths).astype(jnp.int32)


def draw_request_adapter(key, part):
    block_list = REQUESTS // REQUESTS_PER_SLOT
    capacity = 2 * REQUESTS_PER_SLOT // block_list
    slot_total = block_list * capacity
    slot_ids = jnp.arange(slot_total, dtype=jnp.int32)
    slot_owner = slot_ids // capacity
    first_slot = 0
    last_slot = (block_list - 1) * capacity
    hot_owner = jax.random.randint(jax.random.fold_in(key, 41), (block_list,), 0, 4) == 0
    full_owner = jax.random.randint(jax.random.fold_in(key, 42), (), 0, block_list)
    scores = jax.random.randint(jax.random.fold_in(key, 43), (block_list, slot_total), 0, 1 << 20)
    scores = scores + jnp.where(hot_owner[slot_owner], 1 << 20, 0)[None, :]
    scores = scores + jnp.where(slot_owner == full_owner, 1 << 22, 0)[None, :]
    forced_slot = (slot_ids == first_slot) | (slot_ids == last_slot)
    block_zero = jnp.arange(block_list, dtype=jnp.int32) == 0
    scores = scores + jnp.where(block_zero[:, None] & forced_slot[None, :], 1 << 23, 0)
    ranked = jnp.argsort(-scores, axis=1, stable=True)[:, :REQUESTS_PER_SLOT]
    shuffle = jnp.argsort(jax.random.randint(jax.random.fold_in(key, 44), (block_list, REQUESTS_PER_SLOT), 0, 1 << 30), axis=1, stable=True)
    chosen = jnp.take_along_axis(ranked, shuffle, axis=1)
    owners = slot_owner[chosen]
    first_pick = jax.random.randint(jax.random.fold_in(key, 45), (block_list, REQUESTS_PER_SLOT), 0, AD_DEV)
    second_pick = jax.random.randint(jax.random.fold_in(key, 46), (block_list, REQUESTS_PER_SLOT), 0, AD_DEV)
    offsets = jax.random.randint(jax.random.fold_in(key, 47), (block_list,), 0, AD_DEV)
    local_pick = (jnp.minimum(first_pick, second_pick) + offsets[owners]) % AD_DEV
    local_pick = jnp.where(block_zero[:, None] & (chosen == first_slot), 0, local_pick)
    local_pick = jnp.where(block_zero[:, None] & (chosen == last_slot), AD_DEV - 1, local_pick)
    return (owners * AD_DEV + local_pick).reshape(REQUESTS).astype(jnp.int32)


def block_levels(stream_key, dims, shards, least, high):
    def one(dim, shards_of):
        heights = jax.random.uniform(jax.random.fold_in(jax.random.fold_in(stream_key, 6), dim), (shards_of,), jnp.float32, least / len(shards), high / len(shards))
        return jnp.repeat(jnp.exp(heights), dims[dim] // shards_of).reshape((-1,) + (1,) * (len(dims) - dim - 1))

    loudness = one(*shards[0])
    for cut in shards[1:]:
        loudness = loudness * one(*cut)
    return loudness


def noise(rng, shape, deviation, most, shards=(), held_as=jnp.bfloat16):
    entries = jax.random.normal(rng, shape, jnp.float32) * deviation
    if len(shards) > 0:
        entries = block_levels(rng, shape, shards, -0.22, 0.18) * entries
    return jnp.clip(entries, min=-most, max=most).astype(held_as)


def setup_inputs(seed: int = 0) -> dict:
    key_of = jax.random.split(jax.random.key(seed), 11)
    return {
        "hidden": noise(key_of[0], (REQUESTS, NEW_TOKENS, MODEL_DIM), 1.0, 6.0, ((0, 8),)),
        "input_norm_gain": jnp.clip(1.0 + 0.15 * jax.random.normal(key_of[1], (MODEL_DIM,), jnp.float32), 0.25, 1.75).astype(jnp.bfloat16),
        "key_value_weight": noise(key_of[2], (MODEL_DIM, 2, KEY_VALUE_HEADS * HEAD_DIM), MODEL_DIM ** -0.5, 0.0625, ((2, 4),)),
        "adapter_down_weight": noise(key_of[3], (ADAPTER_TOTAL, MODEL_DIM, 2 * ADAPTER_RANK), MODEL_DIM ** -0.5, 0.0625, ((0, 8), (1, 4))),
        "adapter_up_weight": noise(key_of[4], (ADAPTER_TOTAL, 2, ADAPTER_RANK, KEY_VALUE_HEADS * HEAD_DIM), (4 * ADAPTER_RANK) ** -0.5, 0.375, ((0, 8), (3, 4))),
        "request_adapter": draw_request_adapter(jax.random.fold_in(key_of[10], 71), 0),
        "queries": draw_queries(jax.random.fold_in(key_of[10], 71), 0),
        "cached_key_rows": draw_cached_key_rows(jax.random.fold_in(key_of[10], 71), 0),
        "cached_value_rows": noise(key_of[8], (REQUESTS, CTX, KEY_VALUE_HEADS * HEAD_DIM), 1.0, 6.0, ((0, 8), (2, 4))),
        "cached_length": draw_cached_length(jax.random.fold_in(key_of[10], 71), 0),
    }


epsilon = 1e-05
rope_base = 500000.0

def rotate_keys(key_vecs, positions):
    head_size = key_vecs.shape[-1]
    half_size = head_size // 2
    inverse = rope_base ** (-(jnp.arange(half_size, dtype=jnp.float32) * 2.0 / head_size))
    angles = positions[..., None] * inverse
    cosine = jnp.cos(angles)
    sine_part = jnp.sin(angles)
    first_half = key_vecs[..., :half_size]
    second = key_vecs[..., half_size:]
    return jnp.concatenate([first_half * cosine - second * sine_part, second * cosine + first_half * sine_part], axis=-1)

def normalize(hidden, input_norm_gain):
    values = hidden.astype(jnp.float32)
    meansq = lax.optimization_barrier(jnp.mean(values * values, axis=-1, keepdims=True))
    return (values * lax.rsqrt(meansq + epsilon) * input_norm_gain.astype(jnp.float32)).astype(jnp.bfloat16)

def attend(queries, cached_key_rows, cached_value_rows, cached_length, new_keys, new_values):
    score_scale = float(HEAD_DIM) ** (-0.5)
    query_vecs = queries.reshape(REQUESTS, NEW_TOKENS, KEY_VALUE_HEADS, GQ, HEAD_DIM).astype(jnp.float32)
    cache_vecs = cached_key_rows.reshape(REQUESTS, CTX, KEY_VALUE_HEADS, HEAD_DIM).astype(jnp.float32)
    fresh_vecs = new_keys.reshape(REQUESTS, NEW_TOKENS, KEY_VALUE_HEADS, HEAD_DIM).astype(jnp.float32)
    cache_scores = jnp.einsum('rthgd,rjhd->rthgj', query_vecs, cache_vecs) * score_scale
    slot_live = jnp.arange(CTX, dtype=jnp.int32)[None, :] < cached_length[:, None]
    cache_scores = jnp.where(slot_live[:, None, None, None, :], cache_scores, -1e+30)
    fresh_scores = jnp.einsum('rthgd,rshd->rthgs', query_vecs, fresh_vecs) * score_scale
    causal = jnp.arange(NEW_TOKENS, dtype=jnp.int32)[:, None] >= jnp.arange(NEW_TOKENS, dtype=jnp.int32)[None, :]
    fresh_scores = jnp.where(causal[None, :, None, None, :], fresh_scores, -1e+30)
    top_score = jnp.maximum(lax.optimization_barrier(jnp.max(cache_scores, axis=-1)), lax.optimization_barrier(jnp.max(fresh_scores, axis=-1)))[..., None]
    cache_weights = jnp.exp(cache_scores - top_score)
    fresh_weights = jnp.exp(fresh_scores - top_score)
    total_weight = lax.optimization_barrier(jnp.sum(cache_weights, axis=-1, keepdims=True)) + lax.optimization_barrier(jnp.sum(fresh_weights, axis=-1, keepdims=True))
    cache_probs = (cache_weights / total_weight).astype(jnp.bfloat16)
    fresh_probs = (fresh_weights / total_weight).astype(jnp.bfloat16)
    cache_vals = cached_value_rows.reshape(REQUESTS, CTX, KEY_VALUE_HEADS, HEAD_DIM).astype(jnp.float32)
    fresh_vals = new_values.reshape(REQUESTS, NEW_TOKENS, KEY_VALUE_HEADS, HEAD_DIM).astype(jnp.float32)
    mixed_out = jnp.einsum('rthgj,rjhd->rthgd', cache_probs.astype(jnp.float32), cache_vals)
    mixed_out = mixed_out + jnp.einsum('rthgs,rshd->rthgd', fresh_probs.astype(jnp.float32), fresh_vals)
    return mixed_out.reshape(REQUESTS, NEW_TOKENS, KEY_VALUE_HEADS * GQ * HEAD_DIM).astype(jnp.bfloat16)

def reference(hidden, input_norm_gain, key_value_weight, adapter_down_weight, adapter_up_weight, request_adapter, queries, cached_key_rows, cached_value_rows, cached_length):
    normed_input = normalize(hidden, input_norm_gain)
    flat_rows = normed_input.reshape(REQUESTS * NEW_TOKENS, MODEL_DIM)
    base_proj = jnp.dot(flat_rows, key_value_weight.reshape(MODEL_DIM, 2 * KEY_VALUE_HEADS * HEAD_DIM), preferred_element_type=jnp.float32)
    base_proj = base_proj.reshape(REQUESTS, NEW_TOKENS, 2, KEY_VALUE_HEADS * HEAD_DIM)
    block_list = REQUESTS // REQUESTS_PER_SLOT

    def adapter_block(operand_list):
        block_rows, block_numbers = operand_list
        down_matrices = adapter_down_weight[block_numbers].astype(jnp.float32)
        rank_hidden = jnp.einsum('rtd,rdk->rtk', block_rows.astype(jnp.float32), down_matrices).astype(jnp.bfloat16)
        up_matrices = adapter_up_weight[block_numbers].astype(jnp.float32)
        key_part = jnp.einsum('rtk,rkh->rth', rank_hidden[..., :ADAPTER_RANK].astype(jnp.float32), up_matrices[:, 0])
        value_part = jnp.einsum('rtk,rkh->rth', rank_hidden[..., ADAPTER_RANK:].astype(jnp.float32), up_matrices[:, 1])
        return jnp.stack([key_part, value_part], axis=2)
    adapter_update = lax.map(adapter_block, (normed_input.reshape(block_list, REQUESTS_PER_SLOT, NEW_TOKENS, MODEL_DIM), request_adapter.reshape(block_list, REQUESTS_PER_SLOT)))
    projected_output = base_proj + adapter_update.reshape(REQUESTS, NEW_TOKENS, 2, KEY_VALUE_HEADS * HEAD_DIM)
    positions = (cached_length[:, None] + jnp.arange(NEW_TOKENS, dtype=jnp.int32)[None, :]).astype(jnp.float32)
    key_vecs = rotate_keys(projected_output[:, :, 0].reshape(REQUESTS, NEW_TOKENS, KEY_VALUE_HEADS, HEAD_DIM), positions[:, :, None])
    new_keys = key_vecs.reshape(REQUESTS, NEW_TOKENS, KEY_VALUE_HEADS * HEAD_DIM).astype(jnp.bfloat16)
    new_values = projected_output[:, :, 1].astype(jnp.bfloat16)
    attended = attend(queries, cached_key_rows, cached_value_rows, cached_length, new_keys, new_values)
    return (new_keys, new_values, attended)
```

```python
import jax
import jax.numpy as jnp
from jax import lax
from jax.sharding import PartitionSpec as P

HEAD_DIM = 128


epsilon = 1e-05
rope_base = 500000.0


def rotate_keys(key_vecs, positions):
    head_size = key_vecs.shape[-1]
    half_size = head_size // 2
    inverse = rope_base ** (-(jnp.arange(half_size, dtype=jnp.float32) * 2.0 / head_size))
    angles = positions[..., None] * inverse
    cosine = jnp.cos(angles)
    sine_part = jnp.sin(angles)
    first_half = key_vecs[..., :half_size]
    second = key_vecs[..., half_size:]
    return jnp.concatenate(
        [first_half * cosine - second * sine_part, second * cosine + first_half * sine_part],
        axis=-1,
    )


def normalize(hidden, input_norm_gain):
    values = hidden.astype(jnp.float32)
    meansq = jnp.mean(values * values, axis=-1, keepdims=True)
    return (values * lax.rsqrt(meansq + epsilon) * input_norm_gain.astype(jnp.float32)).astype(
        jnp.bfloat16
    )


def route(request_adapter, adapter_number, capacity, owner_total):
    me = lax.axis_index("adapter")
    rows = request_adapter.shape[0]
    relative = jnp.bitwise_xor(request_adapter // adapter_number, me)
    same = relative[:, None] == relative[None, :]
    order = jnp.arange(rows, dtype=jnp.int32)
    earlier = order[None, :] < order[:, None]
    rank = jnp.sum((same & earlier).astype(jnp.int32), axis=1)
    slot = relative * capacity + rank
    places = jnp.arange(owner_total * capacity, dtype=jnp.int32)
    return (places[:, None] == slot[None, :]).astype(jnp.bfloat16)


def exchange(blocks, owner_total):
    received = [blocks[0]]
    for step in range(1, owner_total):
        pairs = [(source, source ^ step) for source in range(owner_total)]
        received.append(lax.ppermute(blocks[step], "adapter", pairs))
    return received


def cache_part(queries, cached_key_rows, cached_value_rows, cached_length):
    row_total, token_total, query_width = queries.shape
    context = cached_key_rows.shape[1]
    kv_local = cached_key_rows.shape[2] // HEAD_DIM
    group_size = query_width // (kv_local * HEAD_DIM)
    score_scale = float(HEAD_DIM) ** (-0.5)
    query_vecs = queries.reshape(row_total, token_total, kv_local, group_size, HEAD_DIM)
    cache_vecs = cached_key_rows.reshape(row_total, context, kv_local, HEAD_DIM)
    cache_vals = cached_value_rows.reshape(row_total, context, kv_local, HEAD_DIM)
    scores = (
        jnp.einsum("rthgd,rjhd->rthgj", query_vecs, cache_vecs, preferred_element_type=jnp.float32)
        * score_scale
    )
    slot_live = jnp.arange(context, dtype=jnp.int32)[None, :] < cached_length[:, None]
    scores = jnp.where(slot_live[:, None, None, None, :], scores, -1e30)
    top = jnp.max(scores, axis=-1, keepdims=True)
    weights = jnp.exp(scores - top)
    total = jnp.sum(weights, axis=-1, keepdims=True)
    mixed = jnp.einsum(
        "rthgj,rjhd->rthgd",
        weights.astype(jnp.bfloat16),
        cache_vals,
        preferred_element_type=jnp.float32,
    )
    return query_vecs, top, total, mixed


def finish(query_vecs, top, total, mixed, new_keys, new_values):
    row_total, token_total, kv_local, group_size, head_size = query_vecs.shape
    score_scale = float(head_size) ** (-0.5)
    fresh_keys = new_keys.reshape(row_total, token_total, kv_local, head_size)
    fresh_vals = new_values.reshape(row_total, token_total, kv_local, head_size)
    scores = (
        jnp.einsum("rthgd,rshd->rthgs", query_vecs, fresh_keys, preferred_element_type=jnp.float32)
        * score_scale
    )
    order = jnp.arange(token_total, dtype=jnp.int32)
    causal = order[:, None] >= order[None, :]
    scores = jnp.where(causal[None, :, None, None, :], scores, -1e30)
    peak = jnp.maximum(top, jnp.max(scores, axis=-1, keepdims=True))
    scale = jnp.exp(top - peak)
    weights = jnp.exp(scores - peak)
    denominator = scale * total + jnp.sum(weights, axis=-1, keepdims=True)
    out = mixed * (scale / denominator)
    probs = weights / denominator
    for s in range(token_total):
        out = out + probs[..., s : s + 1] * fresh_vals[:, None, s, :, None, :].astype(jnp.float32)
    return out.reshape(row_total, token_total, -1).astype(jnp.bfloat16)


def body(
    hidden,
    input_norm_gain,
    key_value_weight,
    adapter_down_weight,
    adapter_up_weight,
    request_adapter,
    queries,
    cached_key_rows,
    cached_value_rows,
    cached_length,
):
    row_count, token_count, model_width = hidden.shape
    feature_total = adapter_down_weight.shape[1]
    adapter_number = adapter_down_weight.shape[0]
    column_count = key_value_weight.shape[2]
    owner_total = lax.axis_size("adapter")
    capacity = 2 * row_count // owner_total
    normed_input = normalize(hidden, input_norm_gain)
    feature_start = lax.axis_index("tensor") * feature_total
    own = lax.dynamic_slice_in_dim(normed_input, feature_start, feature_total, 2)
    selector = route(request_adapter, adapter_number, capacity, owner_total)
    marks = jnp.broadcast_to(
        (request_adapter % adapter_number + 1).astype(jnp.bfloat16)[:, None], (row_count, HEAD_DIM)
    )
    parts = [own[:, t] for t in range(token_count)] + [marks]
    packed = jnp.dot(
        selector, jnp.concatenate(parts, axis=1), preferred_element_type=jnp.float32
    ).astype(jnp.bfloat16)
    blocks = packed.reshape(owner_total, capacity, packed.shape[1])
    received = jnp.concatenate(exchange(blocks, owner_total), axis=0)

    base_proj = jnp.dot(
        normed_input.reshape(row_count * token_count, model_width),
        key_value_weight.reshape(model_width, 2 * column_count),
        preferred_element_type=jnp.float32,
    )
    base_proj = base_proj.reshape(row_count, token_count, 2, column_count)
    query_vecs, top, total, mixed = cache_part(
        queries, cached_key_rows, cached_value_rows, cached_length
    )

    routed = received.shape[0]
    names = received[:, token_count * feature_total].astype(jnp.float32)
    rows = jnp.stack(
        [received[:, t * feature_total : (t + 1) * feature_total] for t in range(token_count)]
    ).reshape(token_count * routed, feature_total)
    owned = jnp.arange(1, adapter_number + 1, dtype=jnp.float32)[None, :] == names[:, None]
    owned = jnp.concatenate([owned] * token_count, axis=0)
    partial = jnp.zeros((token_count * routed, adapter_down_weight.shape[2]), jnp.float32)
    for a in range(adapter_number):
        term = jnp.dot(rows, adapter_down_weight[a], preferred_element_type=jnp.float32)
        partial = partial + jnp.where(owned[:, a : a + 1], term, 0.0)
    low_rank = lax.psum(partial, "tensor").astype(jnp.bfloat16)
    rank_width = adapter_up_weight.shape[2]
    deltas = []
    for kind in range(2):
        half = low_rank[:, kind * rank_width : (kind + 1) * rank_width]
        spread = jnp.concatenate(
            [jnp.where(owned[:, a : a + 1], half, 0) for a in range(adapter_number)], axis=1
        )
        deltas.append(
            jnp.dot(
                spread,
                adapter_up_weight[:, kind].reshape(adapter_number * rank_width, column_count),
                preferred_element_type=jnp.float32,
            ).astype(jnp.bfloat16)
        )
    back = jnp.concatenate(
        [
            deltas[kind][t * routed : (t + 1) * routed]
            for t in range(token_count)
            for kind in range(2)
        ],
        axis=1,
    ).reshape(owner_total, capacity, token_count * 2 * column_count)
    returned = jnp.concatenate(exchange(back, owner_total), axis=0)
    adapter_update = jnp.dot(selector.T, returned, preferred_element_type=jnp.float32)
    projected_output = base_proj + adapter_update.reshape(base_proj.shape)

    positions = (cached_length[:, None] + jnp.arange(token_count, dtype=jnp.int32)[None, :]).astype(
        jnp.float32
    )
    kv_local = column_count // HEAD_DIM
    key_vecs = rotate_keys(
        projected_output[:, :, 0].reshape(row_count, token_count, kv_local, HEAD_DIM),
        positions[:, :, None],
    )
    new_keys = key_vecs.reshape(row_count, token_count, column_count).astype(jnp.bfloat16)
    new_values = projected_output[:, :, 1].astype(jnp.bfloat16)
    attended = finish(query_vecs, top, total, mixed, new_keys, new_values)
    return (new_keys, new_values, attended)


def solution(mesh):
    in_specs = (
        P("adapter", None, None),
        P(),
        P(None, None, "tensor"),
        P("adapter", "tensor", None),
        P("adapter", None, None, "tensor"),
        P("adapter"),
        P("adapter", None, "tensor"),
        P("adapter", None, "tensor"),
        P("adapter", None, "tensor"),
        P("adapter"),
    )
    out_specs = (
        P("adapter", None, "tensor"),
        P("adapter", None, "tensor"),
        P("adapter", None, "tensor"),
    )
    return jax.shard_map(body, mesh=mesh, in_specs=in_specs, out_specs=out_specs, check_vma=False)
```

```python
import functools

import jax
import jax.numpy as jnp
from jax import lax
from jax.experimental import pallas as pl
from jax.experimental.pallas import tpu as pltpu
from jax.sharding import PartitionSpec as P

HEAD_DIM = 128


epsilon = 1e-05
rope_base = 500000.0


def rotate_keys(key_vecs, positions):
    head_size = key_vecs.shape[-1]
    half_size = head_size // 2
    inverse = rope_base ** (-(jnp.arange(half_size, dtype=jnp.float32) * 2.0 / head_size))
    angles = positions[..., None] * inverse
    cosine = jnp.cos(angles)
    sine_part = jnp.sin(angles)
    first_half = key_vecs[..., :half_size]
    second = key_vecs[..., half_size:]
    return jnp.concatenate(
        [first_half * cosine - second * sine_part, second * cosine + first_half * sine_part],
        axis=-1,
    )


def normalize(hidden, input_norm_gain):
    values = hidden.astype(jnp.float32)
    meansq = jnp.mean(values * values, axis=-1, keepdims=True)
    return (values * lax.rsqrt(meansq + epsilon) * input_norm_gain.astype(jnp.float32)).astype(
        jnp.bfloat16
    )


MESH = pl.DeviceIdType.MESH


def route(request_adapter, adapter_number, capacity, owner_total, token_count):
    me = lax.axis_index("adapter")
    rows = request_adapter.shape[0]
    relative = jnp.mod(request_adapter // adapter_number - me, owner_total)
    same = relative[:, None] == relative[None, :]
    order = jnp.arange(rows, dtype=jnp.int32)
    earlier = order[None, :] < order[:, None]
    rank = jnp.sum((same & earlier).astype(jnp.int32), axis=1)
    tokens = jnp.arange(token_count, dtype=jnp.int32)
    place = (relative[None, :] * token_count + tokens[:, None]) * capacity + rank[None, :]
    places = jnp.arange(owner_total * token_count * capacity, dtype=jnp.int32)
    return place.reshape(-1)[:, None] == places[None, :]


def exchange(blocks, owner_total):
    received = {0: blocks[0]}
    middle = owner_total // 2
    for step in sorted(range(1, owner_total), key=lambda step: abs(step - middle)):
        pairs = [(source, (source + step) % owner_total) for source in range(owner_total)]
        received[step] = lax.ppermute(blocks[step], "adapter", pairs)
    return jnp.stack([received[step] for step in range(owner_total)])


def return_kernel(
    owners,
    shards,
    adapters,
    partial_ref,
    names_ref,
    up_ref,
    selector_ref,
    base_ref,
    out_ref,
    parts,
    delta,
    returned,
    part_send,
    part_recv,
    back_send,
    back_recv,
):
    me = lax.axis_index("adapter")
    mine = lax.axis_index("tensor")
    barrier = pltpu.get_barrier_semaphore()
    for step in range(1, owners):
        pl.semaphore_signal(
            barrier, inc=1, device_id=(lax.rem(me + step, owners), mine), device_id_type=MESH
        )
    for step in range(1, shards):
        pl.semaphore_signal(
            barrier, inc=1, device_id=(me, lax.rem(mine + step, shards)), device_id_type=MESH
        )
    pl.semaphore_wait(barrier, owners + shards - 2)

    def part_copy(block, step):
        return pltpu.make_async_remote_copy(
            src_ref=partial_ref.at[block],
            dst_ref=parts.at[step - 1, block],
            send_sem=part_send.at[step - 1, block],
            recv_sem=part_recv.at[step - 1, block],
            device_id=(me, lax.rem(mine + step, shards)),
            device_id_type=MESH,
        )

    def back_copy(block):
        return pltpu.make_async_remote_copy(
            src_ref=delta.at[block],
            dst_ref=returned.at[block],
            send_sem=back_send.at[block],
            recv_sem=back_recv.at[block],
            device_id=(lax.rem(me - block + owners, owners), mine),
            device_id_type=MESH,
        )

    def send_parts(block):
        for step in range(1, shards):
            part_copy(block, step).start()

    def adapter_terms(block):
        total = partial_ref[block]
        for step in range(1, shards):
            part_copy(block, step).wait_recv()
            total = total + parts[step - 1, block]
        names = names_ref[block].astype(jnp.float32)
        spread = jnp.concatenate(
            [jnp.where(names == float(a + 1), total, 0.0) for a in range(adapters)], axis=1
        ).astype(jnp.bfloat16)
        terms = jnp.dot(spread, up_ref[...], preferred_element_type=jnp.float32)
        return terms.astype(jnp.bfloat16)

    @pl.loop(1, owners)
    def _(block):
        send_parts(block)

    send_parts(0)

    @pl.loop(1, owners)
    def _(block):
        delta[block] = adapter_terms(block)
        back_copy(block).start()

    returned[0] = adapter_terms(0)

    @pl.loop(1, owners)
    def _(block):
        back_copy(block).wait_recv()

    rows = returned.shape[0] * returned.shape[1]
    out_ref[...] = base_ref[...] + jnp.dot(
        selector_ref[...],
        returned[...].reshape(rows, returned.shape[2]),
        preferred_element_type=jnp.float32,
    )

    @pl.loop(1, owners)
    def _(block):
        back_copy(block).wait_send()

    @pl.loop(0, owners)
    def _(block):
        for step in range(1, shards):
            part_copy(block, step).wait_send()


def return_terms(partial, names, up_matrix, selector, base, adapters):
    owners, rows, width = partial.shape
    shards = lax.axis_size("tensor")
    columns = base.shape[1]
    return pl.pallas_call(
        functools.partial(return_kernel, owners, shards, adapters),
        out_shape=jax.ShapeDtypeStruct(base.shape, jnp.float32),
        in_specs=[pl.BlockSpec(memory_space=pltpu.VMEM)] * 5,
        out_specs=pl.BlockSpec(memory_space=pltpu.VMEM),
        scratch_shapes=[
            pltpu.VMEM((shards - 1, owners, rows, width), jnp.float32),
            pltpu.VMEM((owners, rows, columns), jnp.bfloat16),
            pltpu.VMEM((owners, rows, columns), jnp.bfloat16),
            pltpu.SemaphoreType.DMA((shards - 1, owners)),
            pltpu.SemaphoreType.DMA((shards - 1, owners)),
            pltpu.SemaphoreType.DMA((owners,)),
            pltpu.SemaphoreType.DMA((owners,)),
        ],
        compiler_params=pltpu.CompilerParams(
            collective_id=0, has_side_effects=True, vmem_limit_bytes=24 * 1024 * 1024
        ),
    )(partial, names, up_matrix, selector, base)


def cache_part(queries, cached_key_rows, cached_value_rows, cached_length):
    row_total, token_total, query_width = queries.shape
    context = cached_key_rows.shape[1]
    kv_local = cached_key_rows.shape[2] // HEAD_DIM
    group_size = query_width // (kv_local * HEAD_DIM)
    score_scale = float(HEAD_DIM) ** (-0.5)
    query_vecs = queries.reshape(row_total, token_total, kv_local, group_size, HEAD_DIM)
    cache_vecs = cached_key_rows.reshape(row_total, context, kv_local, HEAD_DIM)
    cache_vals = cached_value_rows.reshape(row_total, context, kv_local, HEAD_DIM)
    scores = (
        jnp.einsum("rthgd,rjhd->rthgj", query_vecs, cache_vecs, preferred_element_type=jnp.float32)
        * score_scale
    )
    slot_live = jnp.arange(context, dtype=jnp.int32)[None, :] < cached_length[:, None]
    scores = jnp.where(slot_live[:, None, None, None, :], scores, -1e30)
    top = jnp.max(scores, axis=-1, keepdims=True)
    weights = jnp.exp(scores - top)
    total = jnp.sum(weights, axis=-1, keepdims=True)
    mixed = jnp.einsum(
        "rthgj,rjhd->rthgd",
        weights.astype(jnp.bfloat16),
        cache_vals,
        preferred_element_type=jnp.float32,
    )
    return query_vecs, top, total, mixed


def finish(query_vecs, top, total, mixed, new_keys, new_values):
    row_total, token_total, kv_local, group_size, head_size = query_vecs.shape
    score_scale = float(head_size) ** (-0.5)
    fresh_keys = new_keys.reshape(row_total, token_total, kv_local, head_size)
    fresh_vals = new_values.reshape(row_total, token_total, kv_local, head_size)
    scores = (
        jnp.einsum("rthgd,rshd->rthgs", query_vecs, fresh_keys, preferred_element_type=jnp.float32)
        * score_scale
    )
    order = jnp.arange(token_total, dtype=jnp.int32)
    causal = order[:, None] >= order[None, :]
    scores = jnp.where(causal[None, :, None, None, :], scores, -1e30)
    peak = jnp.maximum(top, jnp.max(scores, axis=-1, keepdims=True))
    scale = jnp.exp(top - peak)
    weights = jnp.exp(scores - peak)
    denominator = scale * total + jnp.sum(weights, axis=-1, keepdims=True)
    out = mixed * (scale / denominator)
    probs = weights / denominator
    for s in range(token_total):
        out = out + probs[..., s : s + 1] * fresh_vals[:, None, s, :, None, :].astype(jnp.float32)
    return out.reshape(row_total, token_total, -1).astype(jnp.bfloat16)


def body(
    hidden,
    input_norm_gain,
    key_value_weight,
    adapter_down_weight,
    adapter_up_weight,
    request_adapter,
    queries,
    cached_key_rows,
    cached_value_rows,
    cached_length,
):
    row_count, token_count, model_width = hidden.shape
    feature_total = adapter_down_weight.shape[1]
    adapter_number = adapter_down_weight.shape[0]
    column_count = key_value_weight.shape[2]
    owner_total = lax.axis_size("adapter")
    capacity = -(-(2 * row_count // owner_total) // 8) * 8
    block_rows = token_count * capacity
    normed = normalize(jnp.swapaxes(hidden, 0, 1), input_norm_gain)
    normed = normed.reshape(token_count * row_count, model_width)
    feature_start = lax.axis_index("tensor") * feature_total
    own = lax.dynamic_slice_in_dim(normed, feature_start, feature_total, 1)
    selector = route(request_adapter, adapter_number, capacity, owner_total, token_count)
    selector = selector.astype(jnp.bfloat16)
    marks = jnp.tile((request_adapter % adapter_number + 1).astype(jnp.bfloat16), token_count)
    marks = jnp.broadcast_to(marks[:, None], (token_count * row_count, HEAD_DIM))
    packed = jnp.dot(
        selector.T, jnp.concatenate([own, marks], axis=1), preferred_element_type=jnp.float32
    ).astype(jnp.bfloat16)
    received = exchange(packed.reshape(owner_total, block_rows, packed.shape[1]), owner_total)

    base_proj = jnp.concatenate(
        [
            jnp.dot(normed, key_value_weight[:, kind], preferred_element_type=jnp.float32)
            for kind in range(2)
        ],
        axis=1,
    )
    query_vecs, top, total, mixed = cache_part(
        queries, cached_key_rows, cached_value_rows, cached_length
    )
    rank_width = adapter_up_weight.shape[2]
    zero = jnp.zeros((adapter_number, rank_width, column_count), jnp.bfloat16)
    up_matrix = jnp.concatenate(
        [
            jnp.concatenate([adapter_up_weight[:, 0], zero], axis=2),
            jnp.concatenate([zero, adapter_up_weight[:, 1]], axis=2),
        ],
        axis=1,
    ).reshape(adapter_number * 2 * rank_width, 2 * column_count)
    received, base_proj, up_matrix, query_vecs, top, total, mixed = lax.optimization_barrier(
        (received, base_proj, up_matrix, query_vecs, top, total, mixed)
    )

    rows = received[:, :, :feature_total].reshape(owner_total * block_rows, feature_total)
    names = received[:, :, feature_total:]
    owner_name = names[:, :, :1].reshape(owner_total * block_rows, 1).astype(jnp.float32)
    partial = jnp.zeros((owner_total * block_rows, 2 * rank_width), jnp.float32)
    for a in range(adapter_number):
        term = jnp.dot(rows, adapter_down_weight[a], preferred_element_type=jnp.float32)
        partial = partial + jnp.where(owner_name == float(a + 1), term, 0.0)
    partial = partial.reshape(owner_total, block_rows, 2 * rank_width)
    projected = return_terms(partial, names, up_matrix, selector, base_proj, adapter_number)
    projected_output = jnp.swapaxes(
        projected.reshape(token_count, row_count, 2, column_count), 0, 1
    )

    positions = (cached_length[:, None] + jnp.arange(token_count, dtype=jnp.int32)[None, :]).astype(
        jnp.float32
    )
    kv_local = column_count // HEAD_DIM
    key_vecs = rotate_keys(
        projected_output[:, :, 0].reshape(row_count, token_count, kv_local, HEAD_DIM),
        positions[:, :, None],
    )
    new_keys = key_vecs.reshape(row_count, token_count, column_count).astype(jnp.bfloat16)
    new_values = projected_output[:, :, 1].astype(jnp.bfloat16)
    attended = finish(query_vecs, top, total, mixed, new_keys, new_values)
    return (new_keys, new_values, attended)


def solution(mesh):
    in_specs = (
        P("adapter", None, None),
        P(),
        P(None, None, "tensor"),
        P("adapter", "tensor", None),
        P("adapter", None, None, "tensor"),
        P("adapter"),
        P("adapter", None, "tensor"),
        P("adapter", None, "tensor"),
        P("adapter", None, "tensor"),
        P("adapter"),
    )
    out_specs = (
        P("adapter", None, "tensor"),
        P("adapter", None, "tensor"),
        P("adapter", None, "tensor"),
    )
    return jax.shard_map(body, mesh=mesh, in_specs=in_specs, out_specs=out_specs, check_vma=False)
```

```python
import functools

import jax
import jax.numpy as jnp
from jax import lax
from jax.experimental import pallas as pl
from jax.experimental.pallas import tpu as pltpu
from jax.sharding import PartitionSpec as P

HEAD_DIM = 128


epsilon = 1e-05
rope_base = 500000.0


def rotate_keys(key_vecs, positions):
    head_size = key_vecs.shape[-1]
    half_size = head_size // 2
    inverse = rope_base ** (-(jnp.arange(half_size, dtype=jnp.float32) * 2.0 / head_size))
    angles = positions[..., None] * inverse
    cosine = jnp.cos(angles)
    sine_part = jnp.sin(angles)
    first_half = key_vecs[..., :half_size]
    second = key_vecs[..., half_size:]
    return jnp.concatenate(
        [first_half * cosine - second * sine_part, second * cosine + first_half * sine_part],
        axis=-1,
    )


def normalize(hidden, input_norm_gain):
    values = hidden.astype(jnp.float32)
    meansq = jnp.mean(values * values, axis=-1, keepdims=True)
    return (values * lax.rsqrt(meansq + epsilon) * input_norm_gain.astype(jnp.float32)).astype(
        jnp.bfloat16
    )


MESH = pl.DeviceIdType.MESH


def route(request_adapter, adapter_number, capacity, owner_total, token_count):
    me = lax.axis_index("adapter")
    rows = request_adapter.shape[0]
    relative = jnp.mod(request_adapter // adapter_number - me, owner_total)
    same = relative[:, None] == relative[None, :]
    order = jnp.arange(rows, dtype=jnp.int32)
    earlier = order[None, :] < order[:, None]
    rank = jnp.sum((same & earlier).astype(jnp.int32), axis=1)
    tokens = jnp.arange(token_count, dtype=jnp.int32)
    place = (relative[None, :] * token_count + tokens[:, None]) * capacity + rank[None, :]
    places = jnp.arange(owner_total * token_count * capacity, dtype=jnp.int32)
    return place.reshape(-1)[:, None] == places[None, :]


def send_blocks(blocks, steps, owner_total):
    received = {}
    for step in steps:
        pairs = [(source, (source + step) % owner_total) for source in range(owner_total)]
        received[step] = lax.ppermute(blocks[step], "adapter", pairs)
    return received


def return_kernel(
    owners,
    shards,
    adapters,
    *refs,
):
    blocks = refs[:owners]
    down_ref, up_ref, selector_ref, base_ref, out_ref, partial_ref, names_ref = refs[
        owners : owners + 7
    ]
    parts, delta, returned, part_send, part_recv, back_send, back_recv = refs[owners + 7 :]
    me = lax.axis_index("adapter")
    mine = lax.axis_index("tensor")
    barrier = pltpu.get_barrier_semaphore()
    for step in range(1, owners):
        pl.semaphore_signal(
            barrier, inc=1, device_id=(lax.rem(me + step, owners), mine), device_id_type=MESH
        )
    for step in range(1, shards):
        pl.semaphore_signal(
            barrier, inc=1, device_id=(me, lax.rem(mine + step, shards)), device_id_type=MESH
        )
    pl.semaphore_wait(barrier, owners + shards - 2)

    def part_copy(block, step):
        return pltpu.make_async_remote_copy(
            src_ref=partial_ref.at[block],
            dst_ref=parts.at[step - 1, block],
            send_sem=part_send.at[step - 1, block],
            recv_sem=part_recv.at[step - 1, block],
            device_id=(me, lax.rem(mine + step, shards)),
            device_id_type=MESH,
        )

    def back_copy(block):
        return pltpu.make_async_remote_copy(
            src_ref=delta.at[block],
            dst_ref=returned.at[block],
            send_sem=back_send.at[block],
            recv_sem=back_recv.at[block],
            device_id=(lax.rem(me - block + owners, owners), mine),
            device_id_type=MESH,
        )

    def send_parts(block):
        for step in range(1, shards):
            part_copy(block, step).start()

    def adapter_terms(block):
        total = partial_ref[block]
        for step in range(1, shards):
            part_copy(block, step).wait_recv()
            total = total + parts[step - 1, block]
        names = names_ref[block].astype(jnp.float32)
        spread = jnp.concatenate(
            [jnp.where(names == float(a + 1), total, 0.0) for a in range(adapters)], axis=1
        ).astype(jnp.bfloat16)
        terms = jnp.dot(spread, up_ref[...], preferred_element_type=jnp.float32)
        return terms.astype(jnp.bfloat16)

    features = down_ref.shape[1]
    for block in [*range(1, owners), 0]:
        names = blocks[block][:, features:]
        names_ref[block] = names
        names = names.astype(jnp.float32)
        rows = blocks[block][:, :features]
        total = jnp.zeros(names.shape, jnp.float32)
        for a in range(adapters):
            term = jnp.dot(rows, down_ref[a], preferred_element_type=jnp.float32)
            total = total + jnp.where(names == float(a + 1), term, 0.0)
        partial_ref[block] = total
        send_parts(block)

    @pl.loop(1, owners)
    def _(block):
        delta[block] = adapter_terms(block)
        back_copy(block).start()

    returned[0] = adapter_terms(0)

    @pl.loop(1, owners)
    def _(block):
        back_copy(block).wait_recv()

    rows = returned.shape[0] * returned.shape[1]
    out_ref[...] = base_ref[...] + jnp.dot(
        selector_ref[...],
        returned[...].reshape(rows, returned.shape[2]),
        preferred_element_type=jnp.float32,
    )

    @pl.loop(1, owners)
    def _(block):
        back_copy(block).wait_send()

    @pl.loop(0, owners)
    def _(block):
        for step in range(1, shards):
            part_copy(block, step).wait_send()


def return_terms(blocks, down_weight, up_matrix, selector, base):
    owners = len(blocks)
    rows = blocks[0].shape[0]
    adapters, _, width = down_weight.shape
    shards = lax.axis_size("tensor")
    columns = base.shape[1]
    return pl.pallas_call(
        functools.partial(return_kernel, owners, shards, adapters),
        out_shape=jax.ShapeDtypeStruct(base.shape, jnp.float32),
        in_specs=[pl.BlockSpec(memory_space=pltpu.VMEM)] * (owners + 4),
        out_specs=pl.BlockSpec(memory_space=pltpu.VMEM),
        scratch_shapes=[
            pltpu.VMEM((owners, rows, width), jnp.float32),
            pltpu.VMEM((owners, rows, width), jnp.bfloat16),
            pltpu.VMEM((shards - 1, owners, rows, width), jnp.float32),
            pltpu.VMEM((owners, rows, columns), jnp.bfloat16),
            pltpu.VMEM((owners, rows, columns), jnp.bfloat16),
            pltpu.SemaphoreType.DMA((shards - 1, owners)),
            pltpu.SemaphoreType.DMA((shards - 1, owners)),
            pltpu.SemaphoreType.DMA((owners,)),
            pltpu.SemaphoreType.DMA((owners,)),
        ],
        compiler_params=pltpu.CompilerParams(
            collective_id=0, has_side_effects=True, vmem_limit_bytes=24 * 1024 * 1024
        ),
    )(*blocks, down_weight, up_matrix, selector, base)


def cache_part(queries, cached_key_rows, cached_value_rows, cached_length):
    row_total, token_total, query_width = queries.shape
    context = cached_key_rows.shape[1]
    kv_local = cached_key_rows.shape[2] // HEAD_DIM
    group_size = query_width // (kv_local * HEAD_DIM)
    score_scale = float(HEAD_DIM) ** (-0.5)
    query_vecs = queries.reshape(row_total, token_total, kv_local, group_size, HEAD_DIM)
    cache_vecs = cached_key_rows.reshape(row_total, context, kv_local, HEAD_DIM)
    cache_vals = cached_value_rows.reshape(row_total, context, kv_local, HEAD_DIM)
    scores = (
        jnp.einsum("rthgd,rjhd->rthgj", query_vecs, cache_vecs, preferred_element_type=jnp.float32)
        * score_scale
    )
    slot_live = jnp.arange(context, dtype=jnp.int32)[None, :] < cached_length[:, None]
    scores = jnp.where(slot_live[:, None, None, None, :], scores, -1e30)
    top = jnp.max(scores, axis=-1, keepdims=True)
    weights = jnp.exp(scores - top)
    total = jnp.sum(weights, axis=-1, keepdims=True)
    mixed = jnp.einsum(
        "rthgj,rjhd->rthgd",
        weights.astype(jnp.bfloat16),
        cache_vals,
        preferred_element_type=jnp.float32,
    )
    return query_vecs, top, total, mixed


def finish(query_vecs, top, total, mixed, new_keys, new_values):
    row_total, token_total, kv_local, group_size, head_size = query_vecs.shape
    score_scale = float(head_size) ** (-0.5)
    fresh_keys = new_keys.reshape(row_total, token_total, kv_local, head_size)
    fresh_vals = new_values.reshape(row_total, token_total, kv_local, head_size)
    scores = (
        jnp.einsum("rthgd,rshd->rthgs", query_vecs, fresh_keys, preferred_element_type=jnp.float32)
        * score_scale
    )
    order = jnp.arange(token_total, dtype=jnp.int32)
    causal = order[:, None] >= order[None, :]
    scores = jnp.where(causal[None, :, None, None, :], scores, -1e30)
    peak = jnp.maximum(top, jnp.max(scores, axis=-1, keepdims=True))
    scale = jnp.exp(top - peak)
    weights = jnp.exp(scores - peak)
    denominator = scale * total + jnp.sum(weights, axis=-1, keepdims=True)
    out = mixed * (scale / denominator)
    probs = weights / denominator
    for s in range(token_total):
        out = out + probs[..., s : s + 1] * fresh_vals[:, None, s, :, None, :].astype(jnp.float32)
    return out.reshape(row_total, token_total, -1).astype(jnp.bfloat16)


def body(
    hidden,
    input_norm_gain,
    key_value_weight,
    adapter_down_weight,
    adapter_up_weight,
    request_adapter,
    queries,
    cached_key_rows,
    cached_value_rows,
    cached_length,
):
    row_count, token_count, model_width = hidden.shape
    feature_total = adapter_down_weight.shape[1]
    adapter_number = adapter_down_weight.shape[0]
    column_count = key_value_weight.shape[2]
    owner_total = lax.axis_size("adapter")
    capacity = -(-(2 * row_count // owner_total) // 8) * 8
    block_rows = token_count * capacity
    normed = normalize(jnp.swapaxes(hidden, 0, 1), input_norm_gain)
    normed = normed.reshape(token_count * row_count, model_width)
    feature_start = lax.axis_index("tensor") * feature_total
    own = lax.dynamic_slice_in_dim(normed, feature_start, feature_total, 1)
    selector = route(request_adapter, adapter_number, capacity, owner_total, token_count)
    selector = selector.astype(jnp.bfloat16)
    marks = jnp.tile((request_adapter % adapter_number + 1).astype(jnp.bfloat16), token_count)
    marks = jnp.broadcast_to(marks[:, None], (token_count * row_count, HEAD_DIM))
    packed = jnp.dot(
        selector.T, jnp.concatenate([own, marks], axis=1), preferred_element_type=jnp.float32
    ).astype(jnp.bfloat16)
    blocks = packed.reshape(owner_total, block_rows, packed.shape[1])
    blocks = [blocks[step] for step in range(owner_total)]
    middle = owner_total // 2
    steps = sorted(range(1, owner_total), key=lambda step: abs(step - middle))
    early, late = steps[:5], steps[5:]
    received = send_blocks(blocks, early, owner_total)

    base_proj = jnp.concatenate(
        [
            jnp.dot(normed, key_value_weight[:, kind], preferred_element_type=jnp.float32)
            for kind in range(2)
        ],
        axis=1,
    )
    waiting = {step: blocks[step] for step in late}
    arrived = {step: received[step] for step in early[:2]}
    waiting, arrived, base_proj, queries = lax.optimization_barrier(
        (waiting, arrived, base_proj, queries)
    )
    received.update(arrived)
    received.update(send_blocks(waiting, late, owner_total))
    query_vecs, top, total, mixed = cache_part(
        queries, cached_key_rows, cached_value_rows, cached_length
    )
    rank_width = adapter_up_weight.shape[2]
    zero = jnp.zeros((adapter_number, rank_width, column_count), jnp.bfloat16)
    up_matrix = jnp.concatenate(
        [
            jnp.concatenate([adapter_up_weight[:, 0], zero], axis=2),
            jnp.concatenate([zero, adapter_up_weight[:, 1]], axis=2),
        ],
        axis=1,
    ).reshape(adapter_number * 2 * rank_width, 2 * column_count)
    received, base_proj, up_matrix, query_vecs, top, total, mixed = lax.optimization_barrier(
        (received, base_proj, up_matrix, query_vecs, top, total, mixed)
    )

    received[0] = blocks[0]
    projected = return_terms(
        [received[step] for step in range(owner_total)],
        adapter_down_weight,
        up_matrix,
        selector,
        base_proj,
    )
    projected_output = jnp.swapaxes(
        projected.reshape(token_count, row_count, 2, column_count), 0, 1
    )

    positions = (cached_length[:, None] + jnp.arange(token_count, dtype=jnp.int32)[None, :]).astype(
        jnp.float32
    )
    kv_local = column_count // HEAD_DIM
    key_vecs = rotate_keys(
        projected_output[:, :, 0].reshape(row_count, token_count, kv_local, HEAD_DIM),
        positions[:, :, None],
    )
    new_keys = key_vecs.reshape(row_count, token_count, column_count).astype(jnp.bfloat16)
    new_values = projected_output[:, :, 1].astype(jnp.bfloat16)
    attended = finish(query_vecs, top, total, mixed, new_keys, new_values)
    return (new_keys, new_values, attended)


def solution(mesh):
    in_specs = (
        P("adapter", None, None),
        P(),
        P(None, None, "tensor"),
        P("adapter", "tensor", None),
        P("adapter", None, None, "tensor"),
        P("adapter"),
        P("adapter", None, "tensor"),
        P("adapter", None, "tensor"),
        P("adapter", None, "tensor"),
        P("adapter"),
    )
    out_specs = (
        P("adapter", None, "tensor"),
        P("adapter", None, "tensor"),
        P("adapter", None, "tensor"),
    )
    return jax.shard_map(body, mesh=mesh, in_specs=in_specs, out_specs=out_specs, check_vma=False)
```

```python
import functools

import jax
import jax.numpy as jnp
from jax import lax
from jax.experimental import pallas as pl
from jax.experimental.pallas import tpu as pltpu
from jax.sharding import PartitionSpec as P

HEAD_DIM = 128


epsilon = 1e-05
rope_base = 500000.0


def rotate_keys(key_vecs, positions):
    head_size = key_vecs.shape[-1]
    half_size = head_size // 2
    inverse = rope_base ** (-(jnp.arange(half_size, dtype=jnp.float32) * 2.0 / head_size))
    angles = positions[..., None] * inverse
    cosine = jnp.cos(angles)
    sine_part = jnp.sin(angles)
    first_half = key_vecs[..., :half_size]
    second = key_vecs[..., half_size:]
    return jnp.concatenate(
        [first_half * cosine - second * sine_part, second * cosine + first_half * sine_part],
        axis=-1,
    )


def normalize(hidden, input_norm_gain):
    values = hidden.astype(jnp.float32)
    meansq = jnp.mean(values * values, axis=-1, keepdims=True)
    return (values * lax.rsqrt(meansq + epsilon) * input_norm_gain.astype(jnp.float32)).astype(
        jnp.bfloat16
    )


MESH = pl.DeviceIdType.MESH


def route(request_adapter, adapter_number, capacity, owner_total, token_count):
    me = lax.axis_index("adapter")
    rows = request_adapter.shape[0]
    relative = jnp.mod(request_adapter // adapter_number - me, owner_total)
    same = relative[:, None] == relative[None, :]
    order = jnp.arange(rows, dtype=jnp.int32)
    earlier = order[None, :] < order[:, None]
    rank = jnp.sum((same & earlier).astype(jnp.int32), axis=1)
    tokens = jnp.arange(token_count, dtype=jnp.int32)
    place = (relative[None, :] * token_count + tokens[:, None]) * capacity + rank[None, :]
    places = jnp.arange(owner_total * token_count * capacity, dtype=jnp.int32)
    return place.reshape(-1)[:, None] == places[None, :]


def send_blocks(blocks, steps, owner_total):
    received = {}
    for step in steps:
        pairs = [(source, (source + step) % owner_total) for source in range(owner_total)]
        received[step] = lax.ppermute(blocks[step], "adapter", pairs)
    return received


def return_kernel(
    owners,
    shards,
    adapters,
    *refs,
):
    blocks = refs[:owners]
    down_ref, up_ref, selector_ref, base_ref, out_ref, partial_ref, names_ref = refs[
        owners : owners + 7
    ]
    parts, delta, returned, part_send, part_recv, back_send, back_recv = refs[owners + 7 :]
    me = lax.axis_index("adapter")
    mine = lax.axis_index("tensor")
    barrier = pltpu.get_barrier_semaphore()
    for step in range(1, owners):
        pl.semaphore_signal(
            barrier, inc=1, device_id=(lax.rem(me + step, owners), mine), device_id_type=MESH
        )
    for step in range(1, shards):
        pl.semaphore_signal(
            barrier, inc=1, device_id=(me, lax.rem(mine + step, shards)), device_id_type=MESH
        )
    pl.semaphore_wait(barrier, owners + shards - 2)

    def part_copy(block, step):
        return pltpu.make_async_remote_copy(
            src_ref=partial_ref.at[block],
            dst_ref=parts.at[step - 1, block],
            send_sem=part_send.at[step - 1, block],
            recv_sem=part_recv.at[step - 1, block],
            device_id=(me, lax.rem(mine + step, shards)),
            device_id_type=MESH,
        )

    def back_copy(block):
        return pltpu.make_async_remote_copy(
            src_ref=delta.at[block],
            dst_ref=returned.at[block],
            send_sem=back_send.at[block],
            recv_sem=back_recv.at[block],
            device_id=(lax.rem(me - block + owners, owners), mine),
            device_id_type=MESH,
        )

    def send_parts(block):
        for step in range(1, shards):
            part_copy(block, step).start()

    def adapter_terms(block):
        total = partial_ref[block]
        for step in range(1, shards):
            part_copy(block, step).wait_recv()
            total = total + parts[step - 1, block]
        names = names_ref[block].astype(jnp.float32)
        spread = jnp.concatenate(
            [jnp.where(names == float(a + 1), total, 0.0) for a in range(adapters)], axis=1
        ).astype(jnp.bfloat16)
        terms = jnp.dot(spread, up_ref[...], preferred_element_type=jnp.float32)
        return terms.astype(jnp.bfloat16)

    features = down_ref.shape[1]
    for block in [*range(1, owners), 0]:
        names = blocks[block][:, features:]
        names_ref[block] = names
        names = names.astype(jnp.float32)
        rows = blocks[block][:, :features]
        total = jnp.zeros(names.shape, jnp.float32)
        for a in range(adapters):
            term = jnp.dot(rows, down_ref[a], preferred_element_type=jnp.float32)
            total = total + jnp.where(names == float(a + 1), term, 0.0)
        partial_ref[block] = total
        send_parts(block)

    @pl.loop(1, owners)
    def _(block):
        delta[block] = adapter_terms(block)
        back_copy(block).start()

    returned[0] = adapter_terms(0)

    @pl.loop(1, owners)
    def _(block):
        back_copy(block).wait_recv()

    rows = returned.shape[0] * returned.shape[1]
    out_ref[...] = base_ref[...] + jnp.dot(
        selector_ref[...],
        returned[...].reshape(rows, returned.shape[2]),
        preferred_element_type=jnp.float32,
    )

    @pl.loop(1, owners)
    def _(block):
        back_copy(block).wait_send()

    @pl.loop(0, owners)
    def _(block):
        for step in range(1, shards):
            part_copy(block, step).wait_send()


def return_terms(blocks, down_weight, up_matrix, selector, base):
    owners = len(blocks)
    rows = blocks[0].shape[0]
    adapters, _, width = down_weight.shape
    shards = lax.axis_size("tensor")
    columns = base.shape[1]
    return pl.pallas_call(
        functools.partial(return_kernel, owners, shards, adapters),
        out_shape=jax.ShapeDtypeStruct(base.shape, jnp.float32),
        in_specs=[pl.BlockSpec(memory_space=pltpu.VMEM)] * (owners + 4),
        out_specs=pl.BlockSpec(memory_space=pltpu.VMEM),
        scratch_shapes=[
            pltpu.VMEM((owners, rows, width), jnp.float32),
            pltpu.VMEM((owners, rows, width), jnp.bfloat16),
            pltpu.VMEM((shards - 1, owners, rows, width), jnp.float32),
            pltpu.VMEM((owners, rows, columns), jnp.bfloat16),
            pltpu.VMEM((owners, rows, columns), jnp.bfloat16),
            pltpu.SemaphoreType.DMA((shards - 1, owners)),
            pltpu.SemaphoreType.DMA((shards - 1, owners)),
            pltpu.SemaphoreType.DMA((owners,)),
            pltpu.SemaphoreType.DMA((owners,)),
        ],
        compiler_params=pltpu.CompilerParams(
            collective_id=0, has_side_effects=True, vmem_limit_bytes=24 * 1024 * 1024
        ),
    )(*blocks, down_weight, up_matrix, selector, base)


def cache_part(queries, cached_key_rows, cached_value_rows, cached_length):
    row_total, token_total, query_width = queries.shape
    context = cached_key_rows.shape[1]
    kv_local = cached_key_rows.shape[2] // HEAD_DIM
    group_size = query_width // (kv_local * HEAD_DIM)
    score_scale = float(HEAD_DIM) ** (-0.5)
    query_vecs = queries.reshape(row_total, token_total, kv_local, group_size, HEAD_DIM)
    slot_live = jnp.arange(context, dtype=jnp.int32)[None, :] < cached_length[:, None]
    tops, totals, mixes = [], [], []
    for head in range(kv_local):
        lanes = slice(head * HEAD_DIM, (head + 1) * HEAD_DIM)
        scores = score_scale * jnp.einsum(
            "rtgd,rjd->rtgj",
            query_vecs[:, :, head],
            cached_key_rows[:, :, lanes],
            preferred_element_type=jnp.float32,
        )
        scores = jnp.where(slot_live[:, None, None, :], scores, -1e30)
        top = jnp.max(scores, axis=-1, keepdims=True)
        weights = jnp.exp(scores - top)
        tops.append(top)
        totals.append(jnp.sum(weights, axis=-1, keepdims=True))
        mixes.append(
            jnp.einsum(
                "rtgj,rjd->rtgd",
                weights.astype(jnp.bfloat16),
                cached_value_rows[:, :, lanes],
                preferred_element_type=jnp.float32,
            )
        )
    top, total, mixed = (jnp.stack(heads, axis=2) for heads in (tops, totals, mixes))
    return query_vecs, top, total, mixed


def finish(query_vecs, top, total, mixed, new_keys, new_values):
    row_total, token_total, kv_local, group_size, head_size = query_vecs.shape
    score_scale = float(head_size) ** (-0.5)
    fresh_keys = new_keys.reshape(row_total, token_total, kv_local, head_size)
    fresh_vals = new_values.reshape(row_total, token_total, kv_local, head_size)
    scores = (
        jnp.einsum("rthgd,rshd->rthgs", query_vecs, fresh_keys, preferred_element_type=jnp.float32)
        * score_scale
    )
    order = jnp.arange(token_total, dtype=jnp.int32)
    causal = order[:, None] >= order[None, :]
    scores = jnp.where(causal[None, :, None, None, :], scores, -1e30)
    peak = jnp.maximum(top, jnp.max(scores, axis=-1, keepdims=True))
    scale = jnp.exp(top - peak)
    weights = jnp.exp(scores - peak)
    denominator = scale * total + jnp.sum(weights, axis=-1, keepdims=True)
    out = mixed * (scale / denominator)
    probs = weights / denominator
    for s in range(token_total):
        out = out + probs[..., s : s + 1] * fresh_vals[:, None, s, :, None, :].astype(jnp.float32)
    return out.reshape(row_total, token_total, -1).astype(jnp.bfloat16)


def body(
    hidden,
    input_norm_gain,
    key_value_weight,
    adapter_down_weight,
    adapter_up_weight,
    request_adapter,
    queries,
    cached_key_rows,
    cached_value_rows,
    cached_length,
):
    row_count, token_count, model_width = hidden.shape
    feature_total = adapter_down_weight.shape[1]
    adapter_number = adapter_down_weight.shape[0]
    column_count = key_value_weight.shape[2]
    owner_total = lax.axis_size("adapter")
    capacity = -(-(2 * row_count // owner_total) // 8) * 8
    block_rows = token_count * capacity
    normed = normalize(jnp.swapaxes(hidden, 0, 1), input_norm_gain)
    normed = normed.reshape(token_count * row_count, model_width)
    feature_start = lax.axis_index("tensor") * feature_total
    own = lax.dynamic_slice_in_dim(normed, feature_start, feature_total, 1)
    selector = route(request_adapter, adapter_number, capacity, owner_total, token_count)
    selector = selector.astype(jnp.bfloat16)
    marks = jnp.tile((request_adapter % adapter_number + 1).astype(jnp.bfloat16), token_count)
    marks = jnp.broadcast_to(marks[:, None], (token_count * row_count, HEAD_DIM))
    packed = jnp.dot(
        selector.T, jnp.concatenate([own, marks], axis=1), preferred_element_type=jnp.float32
    ).astype(jnp.bfloat16)
    blocks = packed.reshape(owner_total, block_rows, packed.shape[1])
    blocks = [blocks[step] for step in range(owner_total)]
    middle = owner_total // 2
    steps = sorted(range(1, owner_total), key=lambda step: abs(step - middle))
    early, late = steps[:5], steps[5:]
    received = send_blocks(blocks, early, owner_total)

    base_proj = jnp.concatenate(
        [
            jnp.dot(normed, key_value_weight[:, kind], preferred_element_type=jnp.float32)
            for kind in range(2)
        ],
        axis=1,
    )
    waiting = {step: blocks[step] for step in late}
    arrived = {step: received[step] for step in early[:2]}
    waiting, arrived, base_proj, queries = lax.optimization_barrier(
        (waiting, arrived, base_proj, queries)
    )
    received.update(arrived)
    received.update(send_blocks(waiting, late, owner_total))
    query_vecs, top, total, mixed = cache_part(
        queries, cached_key_rows, cached_value_rows, cached_length
    )
    rank_width = adapter_up_weight.shape[2]
    zero = jnp.zeros((adapter_number, rank_width, column_count), jnp.bfloat16)
    up_matrix = jnp.concatenate(
        [
            jnp.concatenate([adapter_up_weight[:, 0], zero], axis=2),
            jnp.concatenate([zero, adapter_up_weight[:, 1]], axis=2),
        ],
        axis=1,
    ).reshape(adapter_number * 2 * rank_width, 2 * column_count)
    received, base_proj, up_matrix, query_vecs, top, total, mixed = lax.optimization_barrier(
        (received, base_proj, up_matrix, query_vecs, top, total, mixed)
    )

    received[0] = blocks[0]
    projected = return_terms(
        [received[step] for step in range(owner_total)],
        adapter_down_weight,
        up_matrix,
        selector,
        base_proj,
    )
    projected_output = jnp.swapaxes(
        projected.reshape(token_count, row_count, 2, column_count), 0, 1
    )

    positions = (cached_length[:, None] + jnp.arange(token_count, dtype=jnp.int32)[None, :]).astype(
        jnp.float32
    )
    kv_local = column_count // HEAD_DIM
    key_vecs = rotate_keys(
        projected_output[:, :, 0].reshape(row_count, token_count, kv_local, HEAD_DIM),
        positions[:, :, None],
    )
    new_keys = key_vecs.reshape(row_count, token_count, column_count).astype(jnp.bfloat16)
    new_values = projected_output[:, :, 1].astype(jnp.bfloat16)
    attended = finish(query_vecs, top, total, mixed, new_keys, new_values)
    return (new_keys, new_values, attended)


def solution(mesh):
    in_specs = (
        P("adapter", None, None),
        P(),
        P(None, None, "tensor"),
        P("adapter", "tensor", None),
        P("adapter", None, None, "tensor"),
        P("adapter"),
        P("adapter", None, "tensor"),
        P("adapter", None, "tensor"),
        P("adapter", None, "tensor"),
        P("adapter"),
    )
    out_specs = (
        P("adapter", None, "tensor"),
        P("adapter", None, "tensor"),
        P("adapter", None, "tensor"),
    )
    return jax.shard_map(body, mesh=mesh, in_specs=in_specs, out_specs=out_specs, check_vma=False)
```
